512 devices in a mesh: group: 64 (over z, y), local: 8 (over x, core).
Axes of the slice: x: 4, y: 4, z: 16, core: 2. Of those that a mesh axis runs over, the one named last changes fastest.
Arguments:
- tokens: bfloat16 [16384, 2560], P(('group', 'local')), may hold values from -6 to 6
- chosen_groups: int32 [16384, 3], P(('group', 'local')), may hold values from 0 to 15, as said below
- local_picks: int32 [16384, 6], P(('group', 'local')), may hold values from 0 to 7, as said below
- gate_probs: float32 [16384, 6], P(('group', 'local')), may hold values from 0.02 to 0.5
- w_gate: bfloat16 [8, 16384, 2560], P('local', 'group'), may hold values from -0.125 to 0.125
- w_up: bfloat16 [8, 16384, 2560], P('local', 'group'), may hold values from -0.125 to 0.125
- w_down: bfloat16 [8, 16384, 2560], P('local', 'group'), may hold values from -0.1875 to 0.1875
Outputs:
- mixed: bfloat16 [16384, 2560], P(('group', 'local'))
The draws below stay inside these ranges and needn't reach their ends.
Inputs may be any that keep to these rules, and one draw needn't show every extreme that they name: `chosen_groups`: each token's 3 entries are different. Among the 32 tokens of one device (aligned blocks of rows), no routing group is chosen by more than 8 tokens, and some group by exactly 8 in every block. `local_picks`: entries 2 j and 2 j + 1 are different. Among the tokens of one device, no expert (chosen group, index) is used more than 2 times, and some expert exactly 2 times in every block.
All inputs are finite; a program needn't handle non-finite values.
Results may differ from the reference program's by a relative error of at most 0.0058.
Values may be sent and summed in bfloat16 or wider, within the bound.
No kernel may reach another device: no remote copies, remote signals or barrier semaphores. Data moves between devices by JAX's collectives and lax.ppermute only.
A program may use at most 64 MiB of HBM per device.

```python
import math
import jax
import jax.numpy as jnp
from jax import lax

D = 2560
FF = 1024
TOK_DEV = 32
TOP = 6
TOP_GROUPS = 3
SHARDS = 4
LEXP = 8
N_RG = 16
EXPERTS = 128
TOKENS = 16384
CE = 2
N_GROUP = 64
N_LOCAL = 8


def route_block(key):
    keys = jax.random.split(key, 5)
    base = TOP_GROUPS * TOK_DEV // N_RG
    pairing = jax.random.permutation(keys[0], N_RG)
    moved = jax.random.randint(keys[1], (N_RG // 2,), 0, 3).astype(jnp.int32).at[0].set(2)
    counts = jnp.zeros((N_RG,), jnp.int32).at[pairing[0::2]].set(base + moved).at[pairing[1::2]].set(base - moved)
    layout = jax.random.permutation(keys[2], N_RG)
    laid = counts[layout]
    ends = jnp.cumsum(laid)
    starts = ends - laid
    places = jnp.arange(TOP_GROUPS * TOK_DEV, dtype=jnp.int32)
    run = jnp.sum((places[:, None] >= ends[None, :]).astype(jnp.int32), axis=1)
    group_seq = layout[run]
    rank_seq = places - starts[run]
    shuffle = jax.random.permutation(keys[3], TOK_DEV)
    groups = jnp.zeros((TOK_DEV, TOP_GROUPS), jnp.int32).at[shuffle].set(group_seq.reshape(TOP_GROUPS, TOK_DEV).T)
    ranks = jnp.zeros((TOK_DEV, TOP_GROUPS), jnp.int32).at[shuffle].set(rank_seq.reshape(TOP_GROUPS, TOK_DEV).T)
    orders = jax.vmap(lambda inner: jax.random.permutation(inner, LEXP))(jax.random.split(keys[4], N_RG))
    first = orders[groups, 2 * ranks % LEXP]
    second = orders[groups, (2 * ranks + 1) % LEXP]
    picks = jnp.stack([first, second], axis=2).reshape(TOK_DEV, TOP)
    return (groups, picks)


def route_plan(key):
    blocks = jax.random.split(key, TOKENS // TOK_DEV)
    groups, picks = jax.vmap(route_block)(blocks)
    return (groups.reshape(TOKENS, TOP_GROUPS).astype(jnp.int32), picks.reshape(TOKENS, TOP).astype(jnp.int32))


def draw_chosen_groups(key, part):
    return route_plan(key)[0]


def draw_local_picks(key, part):
    return route_plan(key)[1]


def block_scale(stream_key, extent, cuts, low, largest):
    loudness = 1.0
    for dim, blocks in cuts:
        draws = jax.random.uniform(jax.random.fold_in(jax.random.fold_in(stream_key, 6), dim), (blocks,), jnp.float32, low / len(cuts), largest / len(cuts))
        loudness = loudness * jnp.repeat(jnp.exp(draws), extent[dim] // blocks).reshape((-1,) + (1,) * (len(extent) - 1 - dim))
    return loudness


def gaussian(key, shape, scale, reach, cuts=(), kind=jnp.bfloat16):
    values = scale * jax.random.normal(key, shape, jnp.float32)
    if cuts:
        values = values * block_scale(key, shape, cuts, -0.22, 0.18)
    return jnp.clip(values, -reach, reach).astype(kind)


def setup_inputs(seed: int = 0) -> dict:
    key_list = jax.random.split(jax.random.key(seed), 8)
    return {
        "tokens": gaussian(key_list[0], (TOKENS, D), 1.0, 6.0, ((0, 512),)),
        "chosen_groups": draw_chosen_groups(jax.random.fold_in(key_list[7], 71), 0),
        "local_picks": draw_local_picks(jax.random.fold_in(key_list[7], 71), 0),
        "gate_probs": jnp.clip(jnp.exp(math.log(0.5) - 3.218876 * jax.random.uniform(key_list[3], (TOKENS, TOP), jnp.float32) ** block_scale(key_list[3], (TOKENS, TOP), ((0, 512),), -0.2, 0.2)), 0.02, 0.5),
        "w_gate": gaussian(key_list[4], (LEXP, N_RG * FF, D), D ** -0.5, 0.125, ((0, 8), (1, 64))),
        "w_up": gaussian(key_list[5], (LEXP, N_RG * FF, D), D ** -0.5, 0.125, ((0, 8), (1, 64))),
        "w_down": gaussian(key_list[6], (LEXP, N_RG * FF, D), FF ** -0.5, 0.1875, ((0, 8), (1, 64))),
    }


def reference(tokens, chosen_groups, local_picks, gate_probs, w_gate, w_up, w_down):
    total = tokens.shape[0]
    width = tokens.shape[1]
    pick_group = jnp.repeat(chosen_groups, 2, axis=1)
    expert_ids = (pick_group * LEXP + local_picks).reshape(-1).astype(jnp.int32)
    pair_token = jnp.repeat(jnp.arange(total, dtype=jnp.int32), TOP)
    pair_gate = gate_probs.reshape(-1)
    order = jnp.argsort(expert_ids, stable=True).astype(jnp.int32)
    counts = jnp.sum((expert_ids[:, None] == jnp.arange(EXPERTS, dtype=jnp.int32)[None, :]).astype(jnp.int32), axis=0)
    offsets = (jnp.cumsum(counts) - counts).astype(jnp.int32)
    most_rows = N_GROUP * N_LOCAL * CE
    padded_order = jnp.concatenate([order, jnp.zeros((most_rows,), jnp.int32)])
    shard_width = FF // SHARDS
    contract = (((1,), (1,)), ((), ()))

    def one_expert(carry, expert):
        start = offsets[expert]
        chosen = lax.dynamic_slice_in_dim(padded_order, start, most_rows)
        valid = jnp.arange(most_rows, dtype=jnp.int32) < counts[expert]
        owners = pair_token[chosen]
        weights = jnp.where(valid, pair_gate[chosen], jnp.zeros_like(pair_gate[chosen]))
        rows = tokens[owners]
        group_index = (expert // LEXP).astype(jnp.int32)
        local_index = (expert % LEXP).astype(jnp.int32)
        zero = jnp.zeros((), jnp.int32)
        gate_mat = lax.dynamic_slice(w_gate, (local_index, group_index * FF, zero), (1, FF, width))[0]
        up_mat = lax.dynamic_slice(w_up, (local_index, group_index * FF, zero), (1, FF, width))[0]
        down_mat = lax.dynamic_slice(w_down, (local_index, group_index * FF, zero), (1, FF, width))[0]
        gate_part = lax.dot_general(rows, gate_mat, contract, preferred_element_type=jnp.float32)
        up_part = lax.dot_general(rows, up_mat, contract, preferred_element_type=jnp.float32)
        hidden = (jax.nn.silu(gate_part) * up_part).astype(jnp.bfloat16)
        output = jnp.zeros((most_rows, width), jnp.float32)
        for shard in range(SHARDS):
            piece = jnp.dot(hidden[:, shard * shard_width:(shard + 1) * shard_width], down_mat[shard * shard_width:(shard + 1) * shard_width], preferred_element_type=jnp.float32)
            output = output + piece.astype(jnp.bfloat16).astype(jnp.float32)
        carry = carry.at[owners].add(output * weights[:, None])
        return carry, None

    start_sum = jnp.zeros((total, width), jnp.float32)
    combined, unused = lax.scan(one_expert, start_sum, jnp.arange(EXPERTS, dtype=jnp.int32))
    return combined.astype(jnp.bfloat16)
```

```python
import jax
import jax.numpy as jnp
from jax import lax
from jax.sharding import Mesh, PartitionSpec as P

TOP_GROUPS = 3
N_RG = 16
SHARDS = 4
LEXP = 8
CE = 2
CG = 8
META = 128
BF = jnp.bfloat16
F32 = jnp.float32


def strict_before(n):
    return (jnp.arange(n)[:, None] > jnp.arange(n)[None, :]).astype(F32)


def pack(tokens, chosen_groups, local_picks, gate_probs):
    tok, width = tokens.shape
    picks = local_picks.reshape(tok, TOP_GROUPS, 2).astype(F32)
    gates = gate_probs.reshape(tok, TOP_GROUPS, 2)
    here = (chosen_groups[:, :, None] == jnp.arange(N_RG, dtype=jnp.int32)).astype(F32)
    member = jnp.sum(here, axis=1)
    rank = jnp.dot(strict_before(tok), member, precision=lax.Precision.HIGHEST)
    slot = (rank.T[:, None, :] == jnp.arange(CG, dtype=F32)[None, :, None]) & (
        member.T[:, None, :] > 0
    )
    slot = slot.astype(F32)
    values = jnp.concatenate([picks + 1.0, gates], axis=2)
    by_group = jnp.sum(here[:, :, :, None] * values[:, :, None, :], axis=1)
    meta = jnp.sum(slot[:, :, :, None] * by_group.transpose(1, 0, 2)[:, None, :, :], axis=2)
    meta = meta.reshape(N_RG * CG, 4)
    gate = meta[:, 2:]
    high = gate.astype(BF)
    low = (gate - high.astype(F32)).astype(BF)
    least = (gate - high.astype(F32) - low.astype(F32)).astype(BF)
    cols = jnp.concatenate([meta[:, :2].astype(BF), high, low, least], axis=1)
    cols = jnp.pad(cols, ((0, 0), (0, META - cols.shape[1])))
    slot = slot.reshape(N_RG * CG, tok).astype(BF)
    rows = jnp.dot(slot, tokens, preferred_element_type=F32).astype(BF)
    return jnp.concatenate([rows, cols], axis=1), slot


def spread(cols):
    info = cols.astype(F32).reshape(N_RG, CG, -1)
    picks = info[:, :, :2]
    gates = info[:, :, 2:4] + info[:, :, 4:6] + info[:, :, 6:8]
    lanes = jnp.arange(LEXP, dtype=F32) + 1.0
    match = (picks[:, :, :, None] == lanes).astype(F32)
    hit = jnp.sum(match, axis=2)
    weight = jnp.sum(match * gates[:, :, :, None], axis=2)
    rank = jnp.einsum(
        "rs,zsl->zrl", strict_before(CG), hit, precision=lax.Precision.HIGHEST
    )
    place = (rank[:, :, :, None] == jnp.arange(CE, dtype=F32)) & (hit[:, :, :, None] > 0)
    place = place.astype(F32)
    same = jnp.eye(N_RG, dtype=F32)
    chosen = (
        place.transpose(2, 0, 3, 1)[:, :, :, None, :] * same[None, :, None, :, None]
    ).reshape(LEXP * N_RG * CE, N_RG * CG)
    scaled = chosen * weight.transpose(2, 0, 1).reshape(LEXP, 1, N_RG * CG).repeat(
        N_RG * CE, axis=1
    ).reshape(LEXP * N_RG * CE, N_RG * CG)
    return chosen.astype(BF), scaled


def experts(rows, w_gate, w_up, w_down):
    contract = (((1,), (1,)), ((), ()))
    gate_part = lax.dot_general(rows, w_gate, contract, preferred_element_type=F32)
    up_part = lax.dot_general(rows, w_up, contract, preferred_element_type=F32)
    hidden = (jax.nn.silu(gate_part) * up_part).astype(BF)
    return jnp.dot(hidden, w_down, preferred_element_type=F32).astype(BF)


def on_device(tokens, chosen_groups, local_picks, gate_probs, w_gate, w_up, w_down):
    tok, width = tokens.shape
    packed, slot = pack(tokens, chosen_groups, local_picks, gate_probs)
    arrived = lax.all_to_all(packed.reshape(N_RG, CG, -1), "z", 0, 0, tiled=True)
    arrived = arrived.reshape(N_RG * CG, -1)
    chosen, scaled = spread(arrived[:, width : width + 8])
    rows = jnp.dot(chosen, arrived[:, :width], preferred_element_type=F32).astype(BF)
    rows = jnp.broadcast_to(rows.reshape(1, LEXP, -1, width), (SHARDS, LEXP, N_RG * CE, width))
    rows = rows.reshape(SHARDS * LEXP, N_RG * CE, width)
    rows = lax.all_to_all(rows, ("y", "x", "c"), 0, 0, tiled=True)
    outs = experts(rows.reshape(-1, width), w_gate[0], w_up[0], w_down[0])
    outs = outs.reshape(SHARDS * LEXP, N_RG * CE, width)
    outs = lax.all_to_all(outs, ("y", "x", "c"), 0, 0, tiled=True)
    outs = outs.reshape(-1, width)
    high = scaled.astype(BF)
    low = (scaled - high.astype(F32)).astype(BF)
    contract = (((0,), (0,)), ((), ()))
    high = jnp.tile(high, (SHARDS, 1))
    low = jnp.tile(low, (SHARDS, 1))
    both = lax.dot_general(
        jnp.concatenate([high, low], axis=1), outs, contract, preferred_element_type=F32
    )
    mixed = (both[: N_RG * CG] + both[N_RG * CG :]).astype(BF)
    home = lax.all_to_all(mixed.reshape(N_RG, CG, width), "z", 0, 0, tiled=True)
    home = home.reshape(N_RG * CG, width)
    return lax.dot_general(slot, home, contract, preferred_element_type=F32).astype(BF)


def solution(mesh):
    grid = Mesh(mesh.devices.reshape(N_RG, SHARDS, 4, 2), ("z", "y", "x", "c"))
    every = ("z", "y", "x", "c")
    weights = P(("x", "c"), ("z", "y"), None)
    return jax.shard_map(
        on_device,
        mesh=grid,
        in_specs=(P(every, None),) * 4 + (weights,) * 3,
        out_specs=P(every, None),
        check_vma=False,
    )
```

```python
import jax
import jax.numpy as jnp
from jax import lax
from jax.experimental import pallas as pl
from jax.experimental.pallas import tpu as pltpu
from jax.sharding import Mesh, PartitionSpec as P

TOP_GROUPS = 3
N_RG = 16
SHARDS = 4
LEXP = 8
CE = 2
CG = 8
COPIES = 2
META = 128
BF = jnp.bfloat16
F32 = jnp.float32
I32 = jnp.int32
HELD = N_RG * CG
SPREAD = LEXP * N_RG * CE
VMEM = pl.BlockSpec(memory_space=pltpu.VMEM)
ANY = pl.BlockSpec(memory_space=pl.ANY)


def iota(shape, dim):
    return lax.broadcasted_iota(I32, shape, dim)


def column(info, index):
    return info[:, index : index + 1]


def pack_kernel(groups, picks, gates, tokens, *refs):
    weights, (packed, slot), halves, (held, in_sems, out_sems) = refs[:3], refs[3:5], refs[5:7], refs[7:]
    tok, width = tokens.shape
    part = weights[0].shape[1] // 2
    inward, outward = [], []
    for i, weight in enumerate(weights):
        for j, half in enumerate(halves):
            here = held.at[j, pl.ds(i * part, part)]
            sem = in_sems.at[2 * i + j]
            inward.append(pltpu.make_async_copy(weight.at[0, pl.ds(j * part, part)], here, sem))
            there = half.at[pl.ds(i * part, part)]
            outward.append(pltpu.make_async_copy(here, there, out_sems.at[2 * i + j]))
    for copy in inward:
        copy.start()
    shape = (HELD, tok)
    group = iota(shape, 0) // CG
    row = iota(shape, 0) % CG
    heres = [(groups[k : k + 1, :] == group).astype(F32) for k in range(TOP_GROUPS)]
    member = heres[0] + heres[1] + heres[2]
    earlier = (iota((tok, tok), 0) < iota((tok, tok), 1)).astype(BF)
    rank = jnp.dot(member.astype(BF), earlier, preferred_element_type=F32)
    held = member * (rank == row.astype(F32)).astype(F32)
    slot[...] = held.astype(BF)

    def select(values, j):
        total = heres[0] * values[j : j + 1, :]
        for k in range(1, TOP_GROUPS):
            total = total + heres[k] * values[2 * k + j : 2 * k + j + 1, :]
        return jnp.sum(held * total, axis=1, keepdims=True)

    labels = picks[...].astype(F32) + 1.0
    probs = gates[...]
    for arrival, copy in zip(inward, outward):
        arrival.wait()
        copy.start()
    lane = iota((HELD, META), 1)
    cols = jnp.zeros((HELD, META), F32)
    for j in range(2):
        gate = select(probs, j)
        high = gate.astype(BF).astype(F32)
        low = (gate - high).astype(BF).astype(F32)
        least = gate - high - low
        for place, value in ((0, select(labels, j)), (2, high), (4, low), (6, least)):
            cols = jnp.where(lane == place + j, value, cols)
    packed[:, width:] = cols.astype(BF)
    packed[:, :width] = jnp.dot(held.astype(BF), tokens[...], preferred_element_type=F32).astype(BF)
    for copy in outward:
        copy.wait()


def pack(tokens, groups, picks, gates, w_gate, w_up, w_down):
    tok, width = tokens.shape
    part = w_gate.shape[1] // 2
    small = [groups.T, picks.T, gates.T, tokens]
    whole = lambda shape: pl.BlockSpec(shape, lambda i: (0,) * len(shape))
    struct = lambda *shape: jax.ShapeDtypeStruct(shape, BF)
    shapes = (struct(HELD, width + META), struct(HELD, tok))
    return pl.pallas_call(
        pack_kernel,
        grid=(1,),
        out_shape=shapes + (struct(3 * part, width),) * 2,
        in_specs=[whole(array.shape) for array in small] + [ANY] * 3,
        out_specs=tuple(whole(s.shape) for s in shapes) + (ANY,) * 2,
        scratch_shapes=[
            pltpu.VMEM((2, 3 * part, width), BF),
            pltpu.SemaphoreType.DMA((6,)),
            pltpu.SemaphoreType.DMA((6,)),
        ],
        compiler_params=pltpu.CompilerParams(vmem_limit_bytes=60 << 20),
        name="pack",
    )(*small, w_gate, w_up, w_down)


def places(cols):
    info = cols.astype(F32)
    shape = (HELD, SPREAD)
    slot = iota(shape, 1)
    label = (slot // (N_RG * CE) + 1).astype(F32)
    source = (slot // CE) % N_RG
    place = (slot % CE).astype(F32)
    same = (iota(shape, 0) // CG == source).astype(F32)
    one = same * (column(info, 0) == label).astype(F32)
    two = same * (column(info, 1) == label).astype(F32)
    hit = one + two
    earlier = (iota((HELD, HELD), 1) < iota((HELD, HELD), 0)).astype(BF)
    rank = jnp.dot(earlier, hit.astype(BF), preferred_element_type=F32)
    taken = (rank == place).astype(F32)
    gates = [column(info, 2 + j) + column(info, 4 + j) + column(info, 6 + j) for j in range(2)]
    return taken * hit, taken * (one * gates[0] + two * gates[1])


def spread_kernel(arrived, *refs):
    rows = refs[-1]
    width = rows.shape[1]
    chosen, _ = places(arrived[:, width:])
    sent = jnp.dot(
        chosen.T.astype(BF), arrived[:, :width], preferred_element_type=F32
    ).astype(BF)
    for copy in range(COPIES):
        rows[copy * SPREAD : (copy + 1) * SPREAD, :] = sent


def spread(arrived, *after):
    width = arrived.shape[1] - META
    return pl.pallas_call(
        spread_kernel,
        out_shape=jax.ShapeDtypeStruct((COPIES * SPREAD, width), BF),
        in_specs=[VMEM] + [ANY] * len(after),
        out_specs=VMEM,
        compiler_params=pltpu.CompilerParams(vmem_limit_bytes=16 << 20),
        cost_estimate=pl.CostEstimate(
            flops=2 * SPREAD * HELD * width, bytes_accessed=2 * 3 * HELD * width, transcendentals=0
        ),
        name="spread",
    )(arrived, *after)


def combine_kernel(cols, outs, mixed):
    _, scaled = places(cols[...])
    high = scaled.astype(BF)
    low = (scaled - high.astype(F32)).astype(BF)
    both = jnp.concatenate([high, low], axis=0)
    both = jnp.concatenate([both] * COPIES, axis=1)
    total = jnp.dot(both, outs[...], preferred_element_type=F32)
    mixed[...] = (total[:HELD] + total[HELD:]).astype(BF)


def combine(arrived, outs):
    rows, width = outs.shape
    whole = lambda rows: pl.BlockSpec((rows, width), lambda i: (0, 0))
    return pl.pallas_call(
        combine_kernel,
        grid=(1,),
        out_shape=jax.ShapeDtypeStruct((HELD, width), BF),
        in_specs=[pl.BlockSpec((HELD, META), lambda i: (0, width // META)), whole(rows)],
        out_specs=whole(HELD),
        compiler_params=pltpu.CompilerParams(vmem_limit_bytes=24 << 20),
        cost_estimate=pl.CostEstimate(
            flops=4 * rows * HELD * width, bytes_accessed=2 * 5 * HELD * width, transcendentals=0
        ),
        name="combine",
    )(arrived, outs)


def glu(gate_part, up_part):
    return (gate_part / (1.0 + jnp.exp(-gate_part)) * up_part).astype(BF)


def expert_kernel(rows, w_gate, w_up, w_down, first, second, outs, gate, up, down, sems):
    own = w_gate.shape[1]
    part = own // 2
    copies = []
    for i, (weight, here) in enumerate(((w_gate, gate), (w_up, up), (w_down, down))):
        block = pl.ds(i * part, part)
        sources = (weight.at[0], first.at[block], second.at[block])
        places = (pl.ds(0, own), pl.ds(own, part), pl.ds(own + part, part))
        copies.append(
            [
                pltpu.make_async_copy(source, here.at[place], sems.at[3 * i + j])
                for j, (source, place) in enumerate(zip(sources, places))
            ]
        )
    for group in copies:
        for copy in group:
            copy.start()
    contract = (((1,), (1,)), ((), ()))
    for copy in copies[0]:
        copy.wait()
    gate_part = lax.dot_general(rows[...], gate[...], contract, preferred_element_type=F32)
    for copy in copies[1]:
        copy.wait()
    up_part = lax.dot_general(rows[...], up[...], contract, preferred_element_type=F32)
    hidden = glu(gate_part, up_part)
    for copy in copies[2]:
        copy.wait()
    outs[...] = jnp.dot(hidden, down[...], preferred_element_type=F32).astype(BF)


def experts(rows, w_gate, w_up, w_down, first, second):
    width = rows.shape[1]
    hidden = 2 * w_gate.shape[1]
    return pl.pallas_call(
        expert_kernel,
        out_shape=jax.ShapeDtypeStruct(rows.shape, BF),
        in_specs=[VMEM] + [ANY] * 5,
        out_specs=VMEM,
        scratch_shapes=[pltpu.VMEM((hidden, width), BF)] * 3 + [pltpu.SemaphoreType.DMA((9,))],
        compiler_params=pltpu.CompilerParams(vmem_limit_bytes=40 << 20),
        cost_estimate=pl.CostEstimate(
            flops=6 * rows.shape[0] * hidden * width,
            bytes_accessed=6 * hidden * width + 4 * rows.shape[0] * width,
            transcendentals=rows.shape[0] * hidden,
        ),
        name="experts",
    )(rows, w_gate, w_up, w_down, first, second)


def unpack_kernel(slot, home, result):
    contract = (((0,), (0,)), ((), ()))
    result[...] = lax.dot_general(
        slot[...], home[...], contract, preferred_element_type=F32
    ).astype(BF)


def unpack(slot, home):
    return pl.pallas_call(
        unpack_kernel,
        out_shape=jax.ShapeDtypeStruct((slot.shape[1], home.shape[1]), BF),
        in_specs=[VMEM] * 2,
        out_specs=VMEM,
        compiler_params=pltpu.CompilerParams(vmem_limit_bytes=16 << 20),
        name="unpack",
    )(slot, home)


def ring(block, step):
    return lax.ppermute(block, ("h", "v"), [(i, (i + step) % SHARDS) for i in range(SHARDS)])


def along_z(rows):
    shape = rows.shape
    rows = rows.reshape(N_RG, CG, -1)
    return lax.all_to_all(rows, "z", 0, 0, tiled=True).reshape(shape)


def in_plane(rows):
    shape = rows.shape
    rows = rows.reshape(COPIES * LEXP, N_RG * CE, -1)
    return lax.all_to_all(rows, ("h", "x", "c"), 0, 0, tiled=True).reshape(shape)


def on_device(tokens, chosen_groups, local_picks, gate_probs, w_gate, w_up, w_down):
    packed, slot, first, second = pack(
        tokens, chosen_groups, local_picks, gate_probs, w_gate, w_up, w_down
    )
    first = ring(first, -1)
    second = ring(second, 1)
    arrived = lax.cond(lax.axis_index("z") < N_RG, along_z, lambda block: block, packed)
    rows = in_plane(spread(arrived, first, second))
    outs = experts(rows, w_gate, w_up, w_down, first, second)
    mixed = combine(arrived, in_plane(outs))
    return unpack(slot, along_z(mixed))


def solution(mesh):
    grid = Mesh(mesh.devices.reshape(N_RG, 2, 2, 4, 2), ("z", "h", "v", "x", "c"))
    every = ("z", "h", "v", "x", "c")
    weights = P(("x", "c"), ("z", "h", "v"), None)
    return jax.shard_map(
        on_device,
        mesh=grid,
        in_specs=(P(every, None),) * 4 + (weights,) * 3,
        out_specs=P(every, None),
        check_vma=False,
    )
```

```python
import jax
import jax.numpy as jnp
from jax import lax
from jax.experimental import pallas as pl
from jax.experimental.pallas import tpu as pltpu
from jax.sharding import Mesh, PartitionSpec as P

TOP_GROUPS = 3
N_RG = 16
SHARDS = 4
LEXP = 8
CE = 2
CG = 8
COPIES = 2
META = 128
BF = jnp.bfloat16
F32 = jnp.float32
I32 = jnp.int32
HELD = N_RG * CG
SPREAD = LEXP * N_RG * CE
VMEM = pl.BlockSpec(memory_space=pltpu.VMEM)
ANY = pl.BlockSpec(memory_space=pl.ANY)


def iota(shape, dim):
    return lax.broadcasted_iota(I32, shape, dim)


def column(info, index):
    return info[:, index : index + 1]


def find_slots(groups, tok):
    shape = (HELD, tok)
    group = iota(shape, 0) // CG
    row = iota(shape, 0) % CG
    heres = [(groups[k : k + 1, :] == group).astype(F32) for k in range(TOP_GROUPS)]
    member = heres[0] + heres[1] + heres[2]
    earlier = (iota((tok, tok), 0) < iota((tok, tok), 1)).astype(BF)
    rank = jnp.dot(member.astype(BF), earlier, preferred_element_type=F32)
    held = member * (rank == row.astype(F32)).astype(F32)
    return heres, held


def halve_kernel(w_gate, w_up, w_down, first, second, held, in_sems, out_sems):
    part = w_gate.shape[1] // 2
    inward, outward = [], []
    for i, weight in enumerate((w_gate, w_up, w_down)):
        for j, half in enumerate((first, second)):
            here = held.at[j, pl.ds(i * part, part)]
            sem = in_sems.at[2 * i + j]
            inward.append(pltpu.make_async_copy(weight.at[0, pl.ds(j * part, part)], here, sem))
            there = half.at[pl.ds(i * part, part)]
            outward.append(pltpu.make_async_copy(here, there, out_sems.at[2 * i + j]))
    for copy in inward:
        copy.start()
    for arrival, copy in zip(inward, outward):
        arrival.wait()
        copy.start()
    for copy in outward:
        copy.wait()


def halve(w_gate, w_up, w_down):
    _, hidden, width = w_gate.shape
    half = jax.ShapeDtypeStruct((3 * hidden // 2, width), BF)
    return pl.pallas_call(
        halve_kernel,
        out_shape=(half, half),
        in_specs=[ANY] * 3,
        out_specs=(ANY, ANY),
        scratch_shapes=[
            pltpu.VMEM((2,) + half.shape, BF),
            pltpu.SemaphoreType.DMA((6,)),
            pltpu.SemaphoreType.DMA((6,)),
        ],
        compiler_params=pltpu.CompilerParams(vmem_limit_bytes=60 << 20),
        name="halve",
    )(w_gate, w_up, w_down)


def pack_kernel(groups, picks, gates, tokens, *refs):
    packed = refs[-1]
    tok, width = tokens.shape
    heres, held = find_slots(groups, tok)

    def select(values, j):
        total = heres[0] * values[j : j + 1, :]
        for k in range(1, TOP_GROUPS):
            total = total + heres[k] * values[2 * k + j : 2 * k + j + 1, :]
        return jnp.sum(held * total, axis=1, keepdims=True)

    labels = picks[...].astype(F32) + 1.0
    probs = gates[...]
    lane = iota((HELD, META), 1)
    cols = jnp.zeros((HELD, META), F32)
    for j in range(2):
        gate = select(probs, j)
        high = gate.astype(BF).astype(F32)
        low = (gate - high).astype(BF).astype(F32)
        least = gate - high - low
        for place, value in ((0, select(labels, j)), (2, high), (4, low), (6, least)):
            cols = jnp.where(lane == place + j, value, cols)
    packed[:, width:] = cols.astype(BF)
    packed[:, :width] = jnp.dot(held.astype(BF), tokens[...], preferred_element_type=F32).astype(BF)


def pack(tokens, groups, picks, gates, *after):
    tok, width = tokens.shape
    small = [groups.T, picks.T, gates.T, tokens]
    whole = lambda shape: pl.BlockSpec(shape, lambda i: (0,) * len(shape))
    out = jax.ShapeDtypeStruct((HELD, width + META), BF)
    return pl.pallas_call(
        pack_kernel,
        grid=(1,),
        out_shape=out,
        in_specs=[whole(array.shape) for array in small] + [ANY] * len(after),
        out_specs=whole(out.shape),
        compiler_params=pltpu.CompilerParams(vmem_limit_bytes=56 << 20),
        name="pack",
    )(*small, *after)


def slots_kernel(groups, *refs):
    slot = refs[-1]
    slot[...] = find_slots(groups, slot.shape[1])[1].astype(BF)


def slots(groups, *after):
    return pl.pallas_call(
        slots_kernel,
        out_shape=jax.ShapeDtypeStruct((HELD, groups.shape[0]), BF),
        in_specs=[VMEM] + [ANY] * len(after),
        out_specs=VMEM,
        compiler_params=pltpu.CompilerParams(vmem_limit_bytes=8 << 20),
        name="slots",
    )(groups.T, *after)


def places(cols):
    info = cols.astype(F32)
    shape = (HELD, SPREAD)
    slot = iota(shape, 1)
    label = (slot // (N_RG * CE) + 1).astype(F32)
    source = (slot // CE) % N_RG
    place = (slot % CE).astype(F32)
    same = (iota(shape, 0) // CG == source).astype(F32)
    one = same * (column(info, 0) == label).astype(F32)
    two = same * (column(info, 1) == label).astype(F32)
    hit = one + two
    earlier = (iota((HELD, HELD), 1) < iota((HELD, HELD), 0)).astype(BF)
    rank = jnp.dot(earlier, hit.astype(BF), preferred_element_type=F32)
    taken = (rank == place).astype(F32)
    gates = [column(info, 2 + j) + column(info, 4 + j) + column(info, 6 + j) for j in range(2)]
    return taken * hit, taken * (one * gates[0] + two * gates[1])


def spread_kernel(arrived, *refs):
    rows = refs[-1]
    width = rows.shape[1]
    chosen, _ = places(arrived[:, width:])
    sent = jnp.dot(
        chosen.T.astype(BF), arrived[:, :width], preferred_element_type=F32
    ).astype(BF)
    for copy in range(COPIES):
        rows[copy * SPREAD : (copy + 1) * SPREAD, :] = sent


def spread(arrived, *after):
    width = arrived.shape[1] - META
    return pl.pallas_call(
        spread_kernel,
        out_shape=jax.ShapeDtypeStruct((COPIES * SPREAD, width), BF),
        in_specs=[VMEM] + [ANY] * len(after),
        out_specs=VMEM,
        compiler_params=pltpu.CompilerParams(vmem_limit_bytes=16 << 20),
        cost_estimate=pl.CostEstimate(
            flops=2 * SPREAD * HELD * width, bytes_accessed=2 * 3 * HELD * width, transcendentals=0
        ),
        name="spread",
    )(arrived, *after)


def combine_kernel(cols, outs, mixed):
    _, scaled = places(cols[...])
    high = scaled.astype(BF)
    low = (scaled - high.astype(F32)).astype(BF)
    both = jnp.concatenate([high, low], axis=0)
    both = jnp.concatenate([both] * COPIES, axis=1)
    total = jnp.dot(both, outs[...], preferred_element_type=F32)
    mixed[...] = (total[:HELD] + total[HELD:]).astype(BF)


def combine(arrived, outs):
    rows, width = outs.shape
    whole = lambda rows: pl.BlockSpec((rows, width), lambda i: (0, 0))
    return pl.pallas_call(
        combine_kernel,
        grid=(1,),
        out_shape=jax.ShapeDtypeStruct((HELD, width), BF),
        in_specs=[pl.BlockSpec((HELD, META), lambda i: (0, width // META)), whole(rows)],
        out_specs=whole(HELD),
        compiler_params=pltpu.CompilerParams(vmem_limit_bytes=24 << 20),
        cost_estimate=pl.CostEstimate(
            flops=4 * rows * HELD * width, bytes_accessed=2 * 5 * HELD * width, transcendentals=0
        ),
        name="combine",
    )(arrived, outs)


def glu(gate_part, up_part):
    return (gate_part / (1.0 + jnp.exp(-gate_part)) * up_part).astype(BF)


def expert_kernel(rows, w_gate, w_up, w_down, first, second, outs, gate, up, down, sems):
    own = w_gate.shape[1]
    part = own // 2
    copies = []
    for i, (weight, here) in enumerate(((w_gate, gate), (w_up, up), (w_down, down))):
        block = pl.ds(i * part, part)
        sources = (weight.at[0], first.at[block], second.at[block])
        places = (pl.ds(0, own), pl.ds(own, part), pl.ds(own + part, part))
        copies.append(
            [
                pltpu.make_async_copy(source, here.at[place], sems.at[3 * i + j])
                for j, (source, place) in enumerate(zip(sources, places))
            ]
        )
    for group in copies:
        for copy in group:
            copy.start()
    contract = (((1,), (1,)), ((), ()))
    for copy in copies[0]:
        copy.wait()
    gate_part = lax.dot_general(rows[...], gate[...], contract, preferred_element_type=F32)
    for copy in copies[1]:
        copy.wait()
    up_part = lax.dot_general(rows[...], up[...], contract, preferred_element_type=F32)
    hidden = glu(gate_part, up_part)
    for copy in copies[2]:
        copy.wait()
    outs[...] = jnp.dot(hidden, down[...], preferred_element_type=F32).astype(BF)


def experts(rows, w_gate, w_up, w_down, first, second):
    width = rows.shape[1]
    hidden = 2 * w_gate.shape[1]
    return pl.pallas_call(
        expert_kernel,
        out_shape=jax.ShapeDtypeStruct(rows.shape, BF),
        in_specs=[VMEM] + [ANY] * 5,
        out_specs=VMEM,
        scratch_shapes=[pltpu.VMEM((hidden, width), BF)] * 3 + [pltpu.SemaphoreType.DMA((9,))],
        compiler_params=pltpu.CompilerParams(vmem_limit_bytes=40 << 20),
        cost_estimate=pl.CostEstimate(
            flops=6 * rows.shape[0] * hidden * width,
            bytes_accessed=6 * hidden * width + 4 * rows.shape[0] * width,
            transcendentals=rows.shape[0] * hidden,
        ),
        name="experts",
    )(rows, w_gate, w_up, w_down, first, second)


def unpack_kernel(slot, home, result):
    contract = (((0,), (0,)), ((), ()))
    result[...] = lax.dot_general(
        slot[...], home[...], contract, preferred_element_type=F32
    ).astype(BF)


def unpack(slot, home):
    return pl.pallas_call(
        unpack_kernel,
        out_shape=jax.ShapeDtypeStruct((slot.shape[1], home.shape[1]), BF),
        in_specs=[VMEM] * 2,
        out_specs=VMEM,
        compiler_params=pltpu.CompilerParams(vmem_limit_bytes=16 << 20),
        name="unpack",
    )(slot, home)


def ring(block, step):
    return lax.ppermute(block, ("h", "v"), [(i, (i + step) % SHARDS) for i in range(SHARDS)])


def along_z(rows):
    shape = rows.shape
    rows = rows.reshape(N_RG, CG, -1)
    return lax.all_to_all(rows, "z", 0, 0, tiled=True).reshape(shape)


def in_plane(rows):
    shape = rows.shape
    rows = rows.reshape(COPIES * LEXP, N_RG * CE, -1)
    return lax.all_to_all(rows, ("h", "x", "c"), 0, 0, tiled=True).reshape(shape)


def on_device(tokens, chosen_groups, local_picks, gate_probs, w_gate, w_up, w_down):
    first, second = halve(w_gate, w_up, w_down)
    packed = pack(tokens, chosen_groups, local_picks, gate_probs, first, second)
    first = ring(first, -1)
    second = ring(second, 1)
    arrived = lax.cond(lax.axis_index("z") < N_RG, along_z, lambda block: block, packed)
    rows = in_plane(spread(arrived, first, second))
    outs = experts(rows, w_gate, w_up, w_down, first, second)
    mixed = combine(arrived, in_plane(outs))
    return unpack(slots(chosen_groups, mixed), along_z(mixed))


def solution(mesh):
    grid = Mesh(mesh.devices.reshape(N_RG, 2, 2, 4, 2), ("z", "h", "v", "x", "c"))
    every = ("z", "h", "v", "x", "c")
    weights = P(("x", "c"), ("z", "h", "v"), None)
    return jax.shard_map(
        on_device,
        mesh=grid,
        in_specs=(P(every, None),) * 4 + (weights,) * 3,
        out_specs=P(every, None),
        check_vma=False,
    )
```

```python
import jax
import jax.numpy as jnp
from jax import lax
from jax.experimental import pallas as pl
from jax.experimental.pallas import tpu as pltpu
from jax.sharding import Mesh, PartitionSpec as P

TOP_GROUPS = 3
N_RG = 16
SHARDS = 4
LEXP = 8
CE = 2
CG = 8
COPIES = 2
META = 128
BF = jnp.bfloat16
F32 = jnp.float32
I32 = jnp.int32
HELD = N_RG * CG
SPREAD = LEXP * N_RG * CE
VMEM = pl.BlockSpec(memory_space=pltpu.VMEM)
ANY = pl.BlockSpec(memory_space=pl.ANY)


def iota(shape, dim):
    return lax.broadcasted_iota(I32, shape, dim)


def column(info, index):
    return info[:, index : index + 1]


def find_slots(groups, tok):
    shape = (HELD, tok)
    group = iota(shape, 0) // CG
    row = iota(shape, 0) % CG
    heres = [(groups[k : k + 1, :] == group).astype(F32) for k in range(TOP_GROUPS)]
    member = heres[0] + heres[1] + heres[2]
    earlier = (iota((tok, tok), 0) < iota((tok, tok), 1)).astype(BF)
    rank = jnp.dot(member.astype(BF), earlier, preferred_element_type=F32)
    held = member * (rank == row.astype(F32)).astype(F32)
    return heres, held


def stack_kernel(w_gate, w_up, w_down, stacked, held, in_sems, out_sems):
    part = w_gate.shape[1] // 2
    inward, outward = [], []
    for i, weight in enumerate((w_gate, w_up, w_down)):
        for j in range(2):
            block = pl.ds((2 * i + j) * part, part)
            source = weight.at[0, pl.ds(j * part, part)]
            sem = 2 * i + j
            inward.append(pltpu.make_async_copy(source, held.at[block], in_sems.at[sem]))
            outward.append(
                pltpu.make_async_copy(held.at[block], stacked.at[block], out_sems.at[sem])
            )
    for copy in inward:
        copy.start()
    for arrival, copy in zip(inward, outward):
        arrival.wait()
        copy.start()
    for copy in outward:
        copy.wait()


def stack(w_gate, w_up, w_down):
    _, hidden, width = w_gate.shape
    whole = (3 * hidden, width)
    return pl.pallas_call(
        stack_kernel,
        out_shape=jax.ShapeDtypeStruct(whole, BF),
        in_specs=[ANY] * 3,
        out_specs=ANY,
        scratch_shapes=[
            pltpu.VMEM(whole, BF),
            pltpu.SemaphoreType.DMA((6,)),
            pltpu.SemaphoreType.DMA((6,)),
        ],
        compiler_params=pltpu.CompilerParams(vmem_limit_bytes=60 << 20),
        name="stack",
    )(w_gate, w_up, w_down)


def pack_kernel(groups, picks, gates, tokens, *refs):
    packed = refs[-1]
    tok, width = tokens.shape
    heres, held = find_slots(groups, tok)

    def select(values, j):
        total = heres[0] * values[j : j + 1, :]
        for k in range(1, TOP_GROUPS):
            total = total + heres[k] * values[2 * k + j : 2 * k + j + 1, :]
        return jnp.sum(held * total, axis=1, keepdims=True)

    labels = picks[...].astype(F32) + 1.0
    probs = gates[...]
    lane = iota((HELD, META), 1)
    cols = jnp.zeros((HELD, META), F32)
    for j in range(2):
        gate = select(probs, j)
        high = gate.astype(BF).astype(F32)
        low = (gate - high).astype(BF).astype(F32)
        least = gate - high - low
        for place, value in ((0, select(labels, j)), (2, high), (4, low), (6, least)):
            cols = jnp.where(lane == place + j, value, cols)
    packed[:, width:] = cols.astype(BF)
    packed[:, :width] = jnp.dot(held.astype(BF), tokens[...], preferred_element_type=F32).astype(BF)


def pack(tokens, groups, picks, gates, *after):
    tok, width = tokens.shape
    small = [groups.T, picks.T, gates.T, tokens]
    whole = lambda shape: pl.BlockSpec(shape, lambda i: (0,) * len(shape))
    out = jax.ShapeDtypeStruct((HELD, width + META), BF)
    return pl.pallas_call(
        pack_kernel,
        grid=(1,),
        out_shape=out,
        in_specs=[whole(array.shape) for array in small] + [ANY] * len(after),
        out_specs=whole(out.shape),
        compiler_params=pltpu.CompilerParams(vmem_limit_bytes=56 << 20),
        name="pack",
    )(*small, *after)


def slots_kernel(groups, *refs):
    slot = refs[-1]
    slot[...] = find_slots(groups, slot.shape[1])[1].astype(BF)


def slots(groups, *after):
    return pl.pallas_call(
        slots_kernel,
        out_shape=jax.ShapeDtypeStruct((HELD, groups.shape[0]), BF),
        in_specs=[VMEM] + [ANY] * len(after),
        out_specs=VMEM,
        compiler_params=pltpu.CompilerParams(vmem_limit_bytes=8 << 20),
        name="slots",
    )(groups.T, *after)


def places(cols):
    info = cols.astype(F32)
    shape = (HELD, SPREAD)
    slot = iota(shape, 1)
    label = (slot // (N_RG * CE) + 1).astype(F32)
    source = (slot // CE) % N_RG
    place = (slot % CE).astype(F32)
    same = (iota(shape, 0) // CG == source).astype(F32)
    one = same * (column(info, 0) == label).astype(F32)
    two = same * (column(info, 1) == label).astype(F32)
    hit = one + two
    earlier = (iota((HELD, HELD), 1) < iota((HELD, HELD), 0)).astype(BF)
    rank = jnp.dot(earlier, hit.astype(BF), preferred_element_type=F32)
    taken = (rank == place).astype(F32)
    gates = [column(info, 2 + j) + column(info, 4 + j) + column(info, 6 + j) for j in range(2)]
    return taken * hit, taken * (one * gates[0] + two * gates[1])


def spread_kernel(arrived, *refs):
    rows = refs[-1]
    width = rows.shape[1]
    chosen, _ = places(arrived[:, width:])
    sent = jnp.dot(
        chosen.T.astype(BF), arrived[:, :width], preferred_element_type=F32
    ).astype(BF)
    for copy in range(COPIES):
        rows[copy * SPREAD : (copy + 1) * SPREAD, :] = sent


def spread(arrived, *after):
    width = arrived.shape[1] - META
    return pl.pallas_call(
        spread_kernel,
        out_shape=jax.ShapeDtypeStruct((COPIES * SPREAD, width), BF),
        in_specs=[VMEM] + [ANY] * len(after),
        out_specs=VMEM,
        compiler_params=pltpu.CompilerParams(vmem_limit_bytes=16 << 20),
        cost_estimate=pl.CostEstimate(
            flops=2 * SPREAD * HELD * width, bytes_accessed=2 * 3 * HELD * width, transcendentals=0
        ),
        name="spread",
    )(arrived, *after)


def combine_kernel(cols, outs, mixed):
    _, scaled = places(cols[...])
    high = scaled.astype(BF)
    low = (scaled - high.astype(F32)).astype(BF)
    both = jnp.concatenate([high, low], axis=0)
    both = jnp.concatenate([both] * COPIES, axis=1)
    total = jnp.dot(both, outs[...], preferred_element_type=F32)
    mixed[...] = (total[:HELD] + total[HELD:]).astype(BF)


def combine(arrived, outs):
    rows, width = outs.shape
    whole = lambda rows: pl.BlockSpec((rows, width), lambda i: (0, 0))
    return pl.pallas_call(
        combine_kernel,
        grid=(1,),
        out_shape=jax.ShapeDtypeStruct((HELD, width), BF),
        in_specs=[pl.BlockSpec((HELD, META), lambda i: (0, width // META)), whole(rows)],
        out_specs=whole(HELD),
        compiler_params=pltpu.CompilerParams(vmem_limit_bytes=24 << 20),
        cost_estimate=pl.CostEstimate(
            flops=4 * rows * HELD * width, bytes_accessed=2 * 5 * HELD * width, transcendentals=0
        ),
        name="combine",
    )(arrived, outs)


def glu(gate_part, up_part):
    return (gate_part / (1.0 + jnp.exp(-gate_part)) * up_part).astype(BF)


def expert_kernel(rows, w_gate, w_up, w_down, other, outs, gate, up, down, sems):
    own = w_gate.shape[1]
    copies = []
    for i, (weight, here) in enumerate(((w_gate, gate), (w_up, up), (w_down, down))):
        sources = (weight.at[0], other.at[pl.ds(i * own, own)])
        copies.append(
            [
                pltpu.make_async_copy(source, here.at[pl.ds(j * own, own)], sems.at[2 * i + j])
                for j, source in enumerate(sources)
            ]
        )
    for group in copies:
        for copy in group:
            copy.start()
    contract = (((1,), (1,)), ((), ()))
    for copy in copies[0]:
        copy.wait()
    gate_part = lax.dot_general(rows[...], gate[...], contract, preferred_element_type=F32)
    for copy in copies[1]:
        copy.wait()
    up_part = lax.dot_general(rows[...], up[...], contract, preferred_element_type=F32)
    hidden = glu(gate_part, up_part)
    for copy in copies[2]:
        copy.wait()
    outs[...] = jnp.dot(hidden, down[...], preferred_element_type=F32).astype(BF)


def experts(rows, w_gate, w_up, w_down, other):
    width = rows.shape[1]
    hidden = 2 * w_gate.shape[1]
    return pl.pallas_call(
        expert_kernel,
        out_shape=jax.ShapeDtypeStruct(rows.shape, BF),
        in_specs=[VMEM] + [ANY] * 4,
        out_specs=VMEM,
        scratch_shapes=[pltpu.VMEM((hidden, width), BF)] * 3 + [pltpu.SemaphoreType.DMA((6,))],
        compiler_params=pltpu.CompilerParams(vmem_limit_bytes=40 << 20),
        cost_estimate=pl.CostEstimate(
            flops=6 * rows.shape[0] * hidden * width,
            bytes_accessed=6 * hidden * width + 4 * rows.shape[0] * width,
            transcendentals=rows.shape[0] * hidden,
        ),
        name="experts",
    )(rows, w_gate, w_up, w_down, other)


def unpack_kernel(slot, home, result):
    contract = (((0,), (0,)), ((), ()))
    result[...] = lax.dot_general(
        slot[...], home[...], contract, preferred_element_type=F32
    ).astype(BF)


def unpack(slot, home):
    return pl.pallas_call(
        unpack_kernel,
        out_shape=jax.ShapeDtypeStruct((slot.shape[1], home.shape[1]), BF),
        in_specs=[VMEM] * 2,
        out_specs=VMEM,
        compiler_params=pltpu.CompilerParams(vmem_limit_bytes=16 << 20),
        name="unpack",
    )(slot, home)


def from_neighbour(block):
    pairs = [
        (2 * y + core, 2 * ((y + step) % SHARDS) + core)
        for y in range(SHARDS)
        for core, step in ((0, -1), (1, 1))
    ]
    return lax.ppermute(block, ("h", "v", "c"), pairs)


def along_z(rows):
    shape = rows.shape
    rows = rows.reshape(N_RG, CG, -1)
    return lax.all_to_all(rows, "z", 0, 0, tiled=True).reshape(shape)


def in_plane(rows):
    shape = rows.shape
    rows = rows.reshape(COPIES * LEXP, N_RG * CE, -1)
    return lax.all_to_all(rows, ("h", "x", "c"), 0, 0, tiled=True).reshape(shape)


def on_device(tokens, chosen_groups, local_picks, gate_probs, w_gate, w_up, w_down):
    stacked = stack(w_gate, w_up, w_down)
    packed = pack(tokens, chosen_groups, local_picks, gate_probs, stacked)
    other = from_neighbour(stacked)
    arrived = lax.cond(lax.axis_index("z") < N_RG, along_z, lambda block: block, packed)
    rows = in_plane(spread(arrived, other))
    outs = experts(rows, w_gate, w_up, w_down, other)
    mixed = combine(arrived, in_plane(outs))
    return unpack(slots(chosen_groups, mixed), along_z(mixed))


def solution(mesh):
    grid = Mesh(mesh.devices.reshape(N_RG, 2, 2, 4, 2), ("z", "h", "v", "x", "c"))
    every = ("z", "h", "v", "x", "c")
    weights = P(("x", "c"), ("z", "h", "v"), None)
    return jax.shard_map(
        on_device,
        mesh=grid,
        in_specs=(P(every, None),) * 4 + (weights,) * 3,
        out_specs=P(every, None),
        check_vma=False,
    )
```

```python
import jax
import jax.numpy as jnp
from jax import lax
from jax.experimental import pallas as pl
from jax.experimental.pallas import tpu as pltpu
from jax.sharding import Mesh, PartitionSpec as P

TOP_GROUPS = 3
N_RG = 16
SHARDS = 4
LEXP = 8
CE = 2
CG = 8
COPIES = 2
META = 128
BF = jnp.bfloat16
F32 = jnp.float32
I32 = jnp.int32
HELD = N_RG * CG
SPREAD = LEXP * N_RG * CE
VMEM = pl.BlockSpec(memory_space=pltpu.VMEM)
ANY = pl.BlockSpec(memory_space=pl.ANY)


def iota(shape, dim):
    return lax.broadcasted_iota(I32, shape, dim)


def column(info, index):
    return info[:, index : index + 1]


def find_slots(groups, tok):
    shape = (HELD, tok)
    group = iota(shape, 0) // CG
    row = iota(shape, 0) % CG
    heres = [(groups[k : k + 1, :] == group).astype(F32) for k in range(TOP_GROUPS)]
    member = heres[0] + heres[1] + heres[2]
    earlier = (iota((tok, tok), 0) < iota((tok, tok), 1)).astype(BF)
    rank = jnp.dot(member.astype(BF), earlier, preferred_element_type=F32)
    held = member * (rank == row.astype(F32)).astype(F32)
    return heres, held


def pack_kernel(
    groups, picks, gates, tokens, w_up, w_down, packed, stacked, held_weights, in_sems, out_sems
):
    tok, width = tokens.shape
    part = w_up.shape[1] // 2
    inward, outward = [], []
    for i, weight in enumerate((w_up, w_down)):
        for j in range(2):
            block = pl.ds((2 * i + j) * part, part)
            source = weight.at[0, pl.ds(j * part, part)]
            here = held_weights.at[block]
            sem = 2 * i + j
            inward.append(pltpu.make_async_copy(source, here, in_sems.at[sem]))
            outward.append(pltpu.make_async_copy(here, stacked.at[block], out_sems.at[sem]))
    for copy in inward:
        copy.start()
    heres, held = find_slots(groups, tok)

    def select(values, j):
        total = heres[0] * values[j : j + 1, :]
        for k in range(1, TOP_GROUPS):
            total = total + heres[k] * values[2 * k + j : 2 * k + j + 1, :]
        return jnp.sum(held * total, axis=1, keepdims=True)

    labels = picks[...].astype(F32) + 1.0
    probs = gates[...]
    for arrival, copy in zip(inward, outward):
        arrival.wait()
        copy.start()
    lane = iota((HELD, META), 1)
    cols = jnp.zeros((HELD, META), F32)
    for j in range(2):
        gate = select(probs, j)
        high = gate.astype(BF).astype(F32)
        low = (gate - high).astype(BF).astype(F32)
        least = gate - high - low
        for place, value in ((0, select(labels, j)), (2, high), (4, low), (6, least)):
            cols = jnp.where(lane == place + j, value, cols)
    packed[:, width:] = cols.astype(BF)
    packed[:, :width] = jnp.dot(held.astype(BF), tokens[...], preferred_element_type=F32).astype(BF)
    for copy in outward:
        copy.wait()


def pack(tokens, groups, picks, gates, w_up, w_down):
    tok, width = tokens.shape
    small = [groups.T, picks.T, gates.T, tokens]
    whole = lambda shape: pl.BlockSpec(shape, lambda i: (0,) * len(shape))
    out = jax.ShapeDtypeStruct((HELD, width + META), BF)
    stacked = jax.ShapeDtypeStruct((2 * w_up.shape[1], width), BF)
    return pl.pallas_call(
        pack_kernel,
        grid=(1,),
        out_shape=(out, stacked),
        in_specs=[whole(array.shape) for array in small] + [ANY] * 2,
        out_specs=(whole(out.shape), ANY),
        scratch_shapes=[
            pltpu.VMEM(stacked.shape, BF),
            pltpu.SemaphoreType.DMA((4,)),
            pltpu.SemaphoreType.DMA((4,)),
        ],
        compiler_params=pltpu.CompilerParams(vmem_limit_bytes=60 << 20),
        name="pack",
    )(*small, w_up, w_down)


def slots_kernel(groups, *refs):
    slot = refs[-1]
    slot[...] = find_slots(groups, slot.shape[1])[1].astype(BF)


def slots(groups, *after):
    return pl.pallas_call(
        slots_kernel,
        out_shape=jax.ShapeDtypeStruct((HELD, groups.shape[0]), BF),
        in_specs=[VMEM] + [ANY] * len(after),
        out_specs=VMEM,
        compiler_params=pltpu.CompilerParams(vmem_limit_bytes=8 << 20),
        name="slots",
    )(groups.T, *after)


def places(cols):
    info = cols.astype(F32)
    shape = (HELD, SPREAD)
    slot = iota(shape, 1)
    label = (slot // (N_RG * CE) + 1).astype(F32)
    source = (slot // CE) % N_RG
    place = (slot % CE).astype(F32)
    same = (iota(shape, 0) // CG == source).astype(F32)
    one = same * (column(info, 0) == label).astype(F32)
    two = same * (column(info, 1) == label).astype(F32)
    hit = one + two
    earlier = (iota((HELD, HELD), 1) < iota((HELD, HELD), 0)).astype(BF)
    rank = jnp.dot(earlier, hit.astype(BF), preferred_element_type=F32)
    taken = (rank == place).astype(F32)
    gates = [column(info, 2 + j) + column(info, 4 + j) + column(info, 6 + j) for j in range(2)]
    return taken * hit, taken * (one * gates[0] + two * gates[1])


def spread_kernel(arrived, *refs):
    rows = refs[-1]
    width = rows.shape[1]
    chosen, _ = places(arrived[:, width:])
    sent = jnp.dot(
        chosen.T.astype(BF), arrived[:, :width], preferred_element_type=F32
    ).astype(BF)
    for copy in range(COPIES):
        rows[copy * SPREAD : (copy + 1) * SPREAD, :] = sent


def spread(arrived, *after):
    width = arrived.shape[1] - META
    return pl.pallas_call(
        spread_kernel,
        out_shape=jax.ShapeDtypeStruct((COPIES * SPREAD, width), BF),
        in_specs=[VMEM] + [ANY] * len(after),
        out_specs=VMEM,
        compiler_params=pltpu.CompilerParams(vmem_limit_bytes=16 << 20),
        cost_estimate=pl.CostEstimate(
            flops=2 * SPREAD * HELD * width, bytes_accessed=2 * 3 * HELD * width, transcendentals=0
        ),
        name="spread",
    )(arrived, *after)


def combine_kernel(cols, outs, mixed):
    _, scaled = places(cols[...])
    high = scaled.astype(BF)
    low = (scaled - high.astype(F32)).astype(BF)
    both = jnp.concatenate([high, low], axis=0)
    both = jnp.concatenate([both] * COPIES, axis=1)
    total = jnp.dot(both, outs[...], preferred_element_type=F32)
    mixed[...] = (total[:HELD] + total[HELD:]).astype(BF)


def combine(arrived, outs):
    rows, width = outs.shape
    whole = lambda rows: pl.BlockSpec((rows, width), lambda i: (0, 0))
    return pl.pallas_call(
        combine_kernel,
        grid=(1,),
        out_shape=jax.ShapeDtypeStruct((HELD, width), BF),
        in_specs=[pl.BlockSpec((HELD, META), lambda i: (0, width // META)), whole(rows)],
        out_specs=whole(HELD),
        compiler_params=pltpu.CompilerParams(vmem_limit_bytes=24 << 20),
        cost_estimate=pl.CostEstimate(
            flops=4 * rows * HELD * width, bytes_accessed=2 * 5 * HELD * width, transcendentals=0
        ),
        name="combine",
    )(arrived, outs)


def glu(gate_part, up_part):
    return (gate_part / (1.0 + jnp.exp(-gate_part)) * up_part).astype(BF)


def expert_kernel(rows, w_gate, w_up, w_down, other_gate, other, outs, gate, up, down, sems):
    own = w_gate.shape[1]
    copies = []
    for i, (weight, here) in enumerate(((w_gate, gate), (w_up, up), (w_down, down))):
        more = other.at[pl.ds((i - 1) * own, own)] if i else other_gate
        sources = (weight.at[0], more)
        copies.append(
            [
                pltpu.make_async_copy(source, here.at[pl.ds(j * own, own)], sems.at[2 * i + j])
                for j, source in enumerate(sources)
            ]
        )
    for group in copies:
        for copy in group:
            copy.start()
    contract = (((1,), (1,)), ((), ()))
    for copy in copies[0]:
        copy.wait()
    gate_part = lax.dot_general(rows[...], gate[...], contract, preferred_element_type=F32)
    for copy in copies[1]:
        copy.wait()
    up_part = lax.dot_general(rows[...], up[...], contract, preferred_element_type=F32)
    hidden = glu(gate_part, up_part)
    for copy in copies[2]:
        copy.wait()
    outs[...] = jnp.dot(hidden, down[...], preferred_element_type=F32).astype(BF)


def experts(rows, w_gate, w_up, w_down, other_gate, other):
    width = rows.shape[1]
    hidden = 2 * w_gate.shape[1]
    return pl.pallas_call(
        expert_kernel,
        out_shape=jax.ShapeDtypeStruct(rows.shape, BF),
        in_specs=[VMEM] + [ANY] * 5,
        out_specs=VMEM,
        scratch_shapes=[pltpu.VMEM((hidden, width), BF)] * 3 + [pltpu.SemaphoreType.DMA((6,))],
        compiler_params=pltpu.CompilerParams(vmem_limit_bytes=40 << 20),
        cost_estimate=pl.CostEstimate(
            flops=6 * rows.shape[0] * hidden * width,
            bytes_accessed=6 * hidden * width + 4 * rows.shape[0] * width,
            transcendentals=rows.shape[0] * hidden,
        ),
        name="experts",
    )(rows, w_gate, w_up, w_down, other_gate, other)


def unpack_kernel(slot, home, result):
    contract = (((0,), (0,)), ((), ()))
    result[...] = lax.dot_general(
        slot[...], home[...], contract, preferred_element_type=F32
    ).astype(BF)


def unpack(slot, home):
    return pl.pallas_call(
        unpack_kernel,
        out_shape=jax.ShapeDtypeStruct((slot.shape[1], home.shape[1]), BF),
        in_specs=[VMEM] * 2,
        out_specs=VMEM,
        compiler_params=pltpu.CompilerParams(vmem_limit_bytes=16 << 20),
        name="unpack",
    )(slot, home)


def from_neighbour(block):
    pairs = [
        (2 * y + core, 2 * ((y + step) % SHARDS) + core)
        for y in range(SHARDS)
        for core, step in ((0, -1), (1, 1))
    ]
    return lax.ppermute(block, ("h", "v", "c"), pairs)


def along_z(rows):
    shape = rows.shape
    rows = rows.reshape(N_RG, CG, -1)
    return lax.all_to_all(rows, "z", 0, 0, tiled=True).reshape(shape)


def in_plane(rows):
    shape = rows.shape
    rows = rows.reshape(COPIES * LEXP, N_RG * CE, -1)
    return lax.all_to_all(rows, ("h", "x", "c"), 0, 0, tiled=True).reshape(shape)


def on_device(tokens, chosen_groups, local_picks, gate_probs, w_gate, w_up, w_down):
    packed, stacked = pack(tokens, chosen_groups, local_picks, gate_probs, w_up, w_down)
    other = from_neighbour(stacked)
    other_gate = from_neighbour(w_gate[0])
    arrived = lax.cond(lax.axis_index("z") < N_RG, along_z, lambda block: block, packed)
    rows = in_plane(spread(arrived, other_gate, other))
    outs = experts(rows, w_gate, w_up, w_down, other_gate, other)
    mixed = combine(arrived, in_plane(outs))
    return unpack(slots(chosen_groups, mixed), along_z(mixed))


def solution(mesh):
    grid = Mesh(mesh.devices.reshape(N_RG, 2, 2, 4, 2), ("z", "h", "v", "x", "c"))
    every = ("z", "h", "v", "x", "c")
    weights = P(("x", "c"), ("z", "h", "v"), None)
    return jax.shard_map(
        on_device,
        mesh=grid,
        in_specs=(P(every, None),) * 4 + (weights,) * 3,
        out_specs=P(every, None),
        check_vma=False,
    )
```

```python
import jax
import jax.numpy as jnp
from jax import lax
from jax.experimental import pallas as pl
from jax.experimental.pallas import tpu as pltpu
from jax.sharding import Mesh, PartitionSpec as P

TOP_GROUPS = 3
N_RG = 16
SHARDS = 4
LEXP = 8
CE = 2
CG = 8
COPIES = 2
META = 128
BF = jnp.bfloat16
F32 = jnp.float32
I32 = jnp.int32
HELD = N_RG * CG
SPREAD = LEXP * N_RG * CE
VMEM = pl.BlockSpec(memory_space=pltpu.VMEM)
ANY = pl.BlockSpec(memory_space=pl.ANY)


def iota(shape, dim):
    return lax.broadcasted_iota(I32, shape, dim)


def column(info, index):
    return info[:, index : index + 1]


def find_slots(groups, tok):
    shape = (HELD, tok)
    group = iota(shape, 0) // CG
    row = iota(shape, 0) % CG
    heres = [(groups[k : k + 1, :] == group).astype(F32) for k in range(TOP_GROUPS)]
    member = heres[0] + heres[1] + heres[2]
    earlier = (iota((tok, tok), 0) < iota((tok, tok), 1)).astype(BF)
    rank = jnp.dot(member.astype(BF), earlier, preferred_element_type=F32)
    held = member * (rank == row.astype(F32)).astype(F32)
    return heres, held


def stack_kernel(w_up, w_down, stacked, held, in_sems, out_sems):
    part = w_up.shape[1] // 2
    inward, outward = [], []
    for i, weight in enumerate((w_up, w_down)):
        for j in range(2):
            block = pl.ds((2 * i + j) * part, part)
            source = weight.at[0, pl.ds(j * part, part)]
            sem = 2 * i + j
            inward.append(pltpu.make_async_copy(source, held.at[block], in_sems.at[sem]))
            outward.append(
                pltpu.make_async_copy(held.at[block], stacked.at[block], out_sems.at[sem])
            )
    for copy in inward:
        copy.start()
    for arrival, copy in zip(inward, outward):
        arrival.wait()
        copy.start()
    for copy in outward:
        copy.wait()


def stack(w_up, w_down):
    _, hidden, width = w_up.shape
    whole = (2 * hidden, width)
    return pl.pallas_call(
        stack_kernel,
        out_shape=jax.ShapeDtypeStruct(whole, BF),
        in_specs=[ANY] * 2,
        out_specs=ANY,
        scratch_shapes=[
            pltpu.VMEM(whole, BF),
            pltpu.SemaphoreType.DMA((4,)),
            pltpu.SemaphoreType.DMA((4,)),
        ],
        compiler_params=pltpu.CompilerParams(vmem_limit_bytes=60 << 20),
        name="stack",
    )(w_up, w_down)


def pack_kernel(groups, picks, gates, tokens, *refs):
    packed = refs[-1]
    tok, width = tokens.shape
    heres, held = find_slots(groups, tok)

    def select(values, j):
        total = heres[0] * values[j : j + 1, :]
        for k in range(1, TOP_GROUPS):
            total = total + heres[k] * values[2 * k + j : 2 * k + j + 1, :]
        return jnp.sum(held * total, axis=1, keepdims=True)

    labels = picks[...].astype(F32) + 1.0
    probs = gates[...]
    lane = iota((HELD, META), 1)
    cols = jnp.zeros((HELD, META), F32)
    for j in range(2):
        gate = select(probs, j)
        high = gate.astype(BF).astype(F32)
        low = (gate - high).astype(BF).astype(F32)
        least = gate - high - low
        for place, value in ((0, select(labels, j)), (2, high), (4, low), (6, least)):
            cols = jnp.where(lane == place + j, value, cols)
    packed[:, width:] = cols.astype(BF)
    packed[:, :width] = jnp.dot(held.astype(BF), tokens[...], preferred_element_type=F32).astype(BF)


def pack(tokens, groups, picks, gates, *after):
    tok, width = tokens.shape
    small = [groups.T, picks.T, gates.T, tokens]
    whole = lambda shape: pl.BlockSpec(shape, lambda i: (0,) * len(shape))
    out = jax.ShapeDtypeStruct((HELD, width + META), BF)
    return pl.pallas_call(
        pack_kernel,
        grid=(1,),
        out_shape=out,
        in_specs=[whole(array.shape) for array in small] + [ANY] * len(after),
        out_specs=whole(out.shape),
        compiler_params=pltpu.CompilerParams(vmem_limit_bytes=56 << 20),
        name="pack",
    )(*small, *after)


def slots_kernel(groups, *refs):
    slot = refs[-1]
    slot[...] = find_slots(groups, slot.shape[1])[1].astype(BF)


def slots(groups, *after):
    return pl.pallas_call(
        slots_kernel,
        out_shape=jax.ShapeDtypeStruct((HELD, groups.shape[0]), BF),
        in_specs=[VMEM] + [ANY] * len(after),
        out_specs=VMEM,
        compiler_params=pltpu.CompilerParams(vmem_limit_bytes=8 << 20),
        name="slots",
    )(groups.T, *after)


def places(cols):
    info = cols.astype(F32)
    shape = (HELD, SPREAD)
    slot = iota(shape, 1)
    label = (slot // (N_RG * CE) + 1).astype(F32)
    source = (slot // CE) % N_RG
    place = (slot % CE).astype(F32)
    same = (iota(shape, 0) // CG == source).astype(F32)
    one = same * (column(info, 0) == label).astype(F32)
    two = same * (column(info, 1) == label).astype(F32)
    hit = one + two
    earlier = (iota((HELD, HELD), 1) < iota((HELD, HELD), 0)).astype(BF)
    rank = jnp.dot(earlier, hit.astype(BF), preferred_element_type=F32)
    taken = (rank == place).astype(F32)
    gates = [column(info, 2 + j) + column(info, 4 + j) + column(info, 6 + j) for j in range(2)]
    return taken * hit, taken * (one * gates[0] + two * gates[1])


def spread_kernel(arrived, *refs):
    rows = refs[-1]
    width = rows.shape[1]
    chosen, _ = places(arrived[:, width:])
    sent = jnp.dot(
        chosen.T.astype(BF), arrived[:, :width], preferred_element_type=F32
    ).astype(BF)
    for copy in range(COPIES):
        rows[copy * SPREAD : (copy + 1) * SPREAD, :] = sent


def spread(arrived, *after):
    width = arrived.shape[1] - META
    return pl.pallas_call(
        spread_kernel,
        out_shape=jax.ShapeDtypeStruct((COPIES * SPREAD, width), BF),
        in_specs=[VMEM] + [ANY] * len(after),
        out_specs=VMEM,
        compiler_params=pltpu.CompilerParams(vmem_limit_bytes=16 << 20),
        cost_estimate=pl.CostEstimate(
            flops=2 * SPREAD * HELD * width, bytes_accessed=2 * 3 * HELD * width, transcendentals=0
        ),
        name="spread",
    )(arrived, *after)


def combine_kernel(cols, outs, mixed):
    _, scaled = places(cols[...])
    high = scaled.astype(BF)
    low = (scaled - high.astype(F32)).astype(BF)
    both = jnp.concatenate([high, low], axis=0)
    both = jnp.concatenate([both] * COPIES, axis=1)
    total = jnp.dot(both, outs[...], preferred_element_type=F32)
    mixed[...] = (total[:HELD] + total[HELD:]).astype(BF)


def combine(arrived, outs):
    rows, width = outs.shape
    whole = lambda rows: pl.BlockSpec((rows, width), lambda i: (0, 0))
    return pl.pallas_call(
        combine_kernel,
        grid=(1,),
        out_shape=jax.ShapeDtypeStruct((HELD, width), BF),
        in_specs=[pl.BlockSpec((HELD, META), lambda i: (0, width // META)), whole(rows)],
        out_specs=whole(HELD),
        compiler_params=pltpu.CompilerParams(vmem_limit_bytes=24 << 20),
        cost_estimate=pl.CostEstimate(
            flops=4 * rows * HELD * width, bytes_accessed=2 * 5 * HELD * width, transcendentals=0
        ),
        name="combine",
    )(arrived, outs)


def glu(gate_part, up_part):
    return (gate_part / (1.0 + jnp.exp(-gate_part)) * up_part).astype(BF)


def expert_kernel(rows, w_gate, w_up, w_down, other_gate, other, outs, gate, up, down, sems):
    own = w_gate.shape[1]
    copies = []
    for i, (weight, here) in enumerate(((w_gate, gate), (w_up, up), (w_down, down))):
        more = other.at[pl.ds((i - 1) * own, own)] if i else other_gate
        sources = (weight.at[0], more)
        copies.append(
            [
                pltpu.make_async_copy(source, here.at[pl.ds(j * own, own)], sems.at[2 * i + j])
                for j, source in enumerate(sources)
            ]
        )
    for group in copies:
        for copy in group:
            copy.start()
    contract = (((1,), (1,)), ((), ()))
    for copy in copies[0]:
        copy.wait()
    gate_part = lax.dot_general(rows[...], gate[...], contract, preferred_element_type=F32)
    for copy in copies[1]:
        copy.wait()
    up_part = lax.dot_general(rows[...], up[...], contract, preferred_element_type=F32)
    hidden = glu(gate_part, up_part)
    for copy in copies[2]:
        copy.wait()
    outs[...] = jnp.dot(hidden, down[...], preferred_element_type=F32).astype(BF)


def experts(rows, w_gate, w_up, w_down, other_gate, other):
    width = rows.shape[1]
    hidden = 2 * w_gate.shape[1]
    return pl.pallas_call(
        expert_kernel,
        out_shape=jax.ShapeDtypeStruct(rows.shape, BF),
        in_specs=[VMEM] + [ANY] * 5,
        out_specs=VMEM,
        scratch_shapes=[pltpu.VMEM((hidden, width), BF)] * 3 + [pltpu.SemaphoreType.DMA((6,))],
        compiler_params=pltpu.CompilerParams(vmem_limit_bytes=40 << 20),
        cost_estimate=pl.CostEstimate(
            flops=6 * rows.shape[0] * hidden * width,
            bytes_accessed=6 * hidden * width + 4 * rows.shape[0] * width,
            transcendentals=rows.shape[0] * hidden,
        ),
        name="experts",
    )(rows, w_gate, w_up, w_down, other_gate, other)


def unpack_kernel(slot, home, result):
    contract = (((0,), (0,)), ((), ()))
    result[...] = lax.dot_general(
        slot[...], home[...], contract, preferred_element_type=F32
    ).astype(BF)


def unpack(slot, home):
    return pl.pallas_call(
        unpack_kernel,
        out_shape=jax.ShapeDtypeStruct((slot.shape[1], home.shape[1]), BF),
        in_specs=[VMEM] * 2,
        out_specs=VMEM,
        compiler_params=pltpu.CompilerParams(vmem_limit_bytes=16 << 20),
        name="unpack",
    )(slot, home)


def from_neighbour(block):
    pairs = [
        (2 * y + core, 2 * ((y + step) % SHARDS) + core)
        for y in range(SHARDS)
        for core, step in ((0, -1), (1, 1))
    ]
    return lax.ppermute(block, ("h", "v", "c"), pairs)


def along_z(rows):
    shape = rows.shape
    rows = rows.reshape(N_RG, CG, -1)
    return lax.all_to_all(rows, "z", 0, 0, tiled=True).reshape(shape)


def in_plane(rows):
    shape = rows.shape
    rows = rows.reshape(COPIES * LEXP, N_RG * CE, -1)
    return lax.all_to_all(rows, ("h", "x", "c"), 0, 0, tiled=True).reshape(shape)


def on_device(tokens, chosen_groups, local_picks, gate_probs, w_gate, w_up, w_down):
    stacked = stack(w_up, w_down)
    packed = pack(tokens, chosen_groups, local_picks, gate_probs, stacked)
    other = from_neighbour(stacked)
    other_gate = from_neighbour(w_gate[0])
    arrived = lax.cond(lax.axis_index("z") < N_RG, along_z, lambda block: block, packed)
    rows = in_plane(spread(arrived, other_gate, other))
    outs = experts(rows, w_gate, w_up, w_down, other_gate, other)
    mixed = combine(arrived, in_plane(outs))
    return unpack(slots(chosen_groups, mixed), along_z(mixed))


def solution(mesh):
    grid = Mesh(mesh.devices.reshape(N_RG, 2, 2, 4, 2), ("z", "h", "v", "x", "c"))
    every = ("z", "h", "v", "x", "c")
    weights = P(("x", "c"), ("z", "h", "v"), None)
    return jax.shard_map(
        on_device,
        mesh=grid,
        in_specs=(P(every, None),) * 4 + (weights,) * 3,
        out_specs=P(every, None),
        check_vma=False,
    )
```
